512 devices in a mesh: grp: 8 (over z), orb: 8 (over y_lo, core), slab: 8 (over x, y_hi).
Axes of the slice: x: 4, y: 8 (y_hi: 2, y_lo: 4; y = y_hi * 4 + y_lo), z: 8, core: 2. Of those that a mesh axis runs over, the one named last changes fastest.
Arguments:
- orbitals: float32 [512, 64, 64, 64], P(('grp', 'orb'), 'slab'), may hold values from -6 to 6
- offsets: int32 [512, 2], replicated, may hold values from 0 to 15
- pairs: int32 [512, 2], P(('grp', 'orb')), may hold values from 0 to 511, as said below
- live: int32 [512], P(('grp', 'orb')), may hold values from 0 to 1, as said below
Outputs:
- exchange: float32 [512, 64, 64, 64], P(('grp', 'orb'), 'slab')
The draws below stay inside these ranges and needn't reach their ends.
Inputs may be any that keep to these rules, and one draw needn't show every extreme that they name: The 8 rows of one device of grp and orb (aligned blocks, in order) name as first orbital one of that device's 8 orbitals; the second orbital lies within 8 positions of the first on the cycle of 512 orbitals. In every block, row 0 pairs the device's lowest orbital with the orbital just below it on the cycle, and row 1 pairs the device's highest orbital with the orbital just above it. In each aligned block of 8 slots the live ones come first, at least two are live, and some block is all live.
All inputs are finite; a program needn't handle non-finite values.
Results may differ from the reference program's by a relative error of at most 0.0003.
Values sent between devices are 32-bit elements; how exact they have to be, the bound alone decides.
No kernel may reach another device: no remote copies, remote signals or barrier semaphores. Data moves between devices by JAX's collectives and lax.ppermute only.
A program may use at most 64 MiB of HBM per device.

```python
import jax
import jax.numpy as jnp
from jax import lax

BOX = 64
MAXOFF = 16
PASSES = 8
ORB_DEV = 8
PAIR_DEV = 8
NORB = 512
PAIRS = 512


def draw_pairs(key, part):
    base = jax.random.fold_in(key, 7)
    key_one, key_two = jax.random.split(base)
    owner = jnp.arange(PAIRS, dtype=jnp.int32) // PAIR_DEV
    slot = jnp.arange(PAIRS, dtype=jnp.int32) % PAIR_DEV
    pick = jax.random.randint(key_one, (PAIRS,), 0, ORB_DEV, dtype=jnp.int32)
    pick = jnp.where(slot == 0, 0, jnp.where(slot == 1, ORB_DEV - 1, pick))
    first = owner * ORB_DEV + pick
    step = jax.random.randint(key_two, (PAIRS,), -ORB_DEV, ORB_DEV + 1, dtype=jnp.int32)
    step = jnp.where(slot == 0, -1, jnp.where(slot == 1, 1, step))
    second = jnp.mod(first + step, NORB)
    return jnp.stack([first, second], axis=1).astype(jnp.int32)


def draw_live(key, part):
    base = jax.random.fold_in(key, 11)
    key_one, key_two = jax.random.split(base)
    blocks = PAIRS // PAIR_DEV
    drawn = jax.random.randint(key_one, (blocks,), 0, PAIR_DEV, dtype=jnp.int32)
    counts = jnp.minimum(2 + drawn * drawn // PAIR_DEV, PAIR_DEV)
    fullest = jax.random.randint(key_two, (), 0, blocks, dtype=jnp.int32)
    counts = jnp.where(jnp.arange(blocks, dtype=jnp.int32) == fullest, PAIR_DEV, counts)
    slots = jnp.arange(PAIRS, dtype=jnp.int32) % PAIR_DEV
    return (slots < jnp.repeat(counts, PAIR_DEV)).astype(jnp.int32)


def set_ends(values, stream_key, smallest, largest):
    longest = values.shape.index(max(values.shape))
    spots = []
    for shift in (0, 1):
        where = [jax.random.randint(jax.random.fold_in(stream_key, axis), (), 0, length) for axis, length in enumerate(values.shape)]
        where[longest] = (where[longest] + shift) % values.shape[longest]
        spots.append(tuple(where))
    return values.at[spots[0]].set(smallest).at[spots[1]].set(largest)


def shard_levels(own_key, shape, pieces, low, largest):
    def one(position, blocks):
        heights = jax.random.uniform(jax.random.fold_in(jax.random.fold_in(own_key, 6), position), (blocks,), jnp.float32, low / len(pieces), largest / len(pieces))
        return jnp.repeat(jnp.exp(heights), shape[position] // blocks).reshape((-1,) + (1,) * (len(shape) - position - 1))

    level = one(*pieces[0])
    for cut in pieces[1:]:
        level = level * one(*cut)
    return level


def noise(rng, shape, width, most, pieces=(), kind=jnp.bfloat16):
    entries = width * jax.random.normal(rng, shape, jnp.float32)
    if pieces:
        entries = entries * shard_levels(rng, shape, pieces, -0.22, 0.18)
    return jnp.clip(entries, -most, most).astype(kind)


def setup_inputs(seed: int = 0) -> dict:
    splits = jax.random.split(jax.random.key(seed), 5)
    orbitals = noise(splits[0], (NORB, BOX, BOX, BOX), 1.0, 6.0, ((0, 64), (1, 8)), jnp.float32)
    offsets = set_ends(jax.random.randint(splits[1], (NORB, 2), 0, MAXOFF), jax.random.fold_in(splits[1], 1), 0, MAXOFF - 1).astype(jnp.int32)
    pairs = draw_pairs(jax.random.fold_in(splits[4], 71), 0)
    live = draw_live(jax.random.fold_in(splits[4], 71), 0)
    return {"orbitals": orbitals, "offsets": offsets, "pairs": pairs, "live": live}


DIAG = 6.25
THETA = 1.075
DELTA = 0.925


def place(field, shift_y, shift_z):
    lead = field.ndim - 2
    padded = jnp.pad(field, [(0, 0)] * lead + [(MAXOFF, MAXOFF), (MAXOFF, MAXOFF)])
    zero = jnp.zeros((), jnp.int32)
    starts = [zero] * lead + [(MAXOFF - shift_y).astype(jnp.int32), (MAXOFF - shift_z).astype(jnp.int32)]
    return lax.dynamic_slice(padded, starts, field.shape)


def apply_op(padded):
    core = padded[:, 1:-1]
    wider = jnp.pad(core, ((0, 0), (0, 0), (1, 1), (1, 1)))
    near = padded[:, 2:] + padded[:, :-2]
    near = near + wider[:, :, 2:, 1:-1] + wider[:, :, :-2, 1:-1]
    near = near + wider[:, :, 1:-1, 2:] + wider[:, :, 1:-1, :-2]
    return DIAG * core - near


def smooth(density, widen):
    sigma = THETA / DELTA
    resid = density
    value = jnp.zeros_like(density)
    step = resid / (DIAG * THETA)
    coef = 1.0 / sigma
    for turn in range(PASSES):
        value = value + step
        if turn < PASSES - 1:
            resid = resid - apply_op(widen(step))
            coef_new = 1.0 / (2.0 * sigma - coef)
            step = (coef_new * coef) * step + (2.0 * coef_new / DELTA) * (resid / DIAG)
            coef = coef_new
    return value


def pad_first(field):
    return jnp.pad(field, ((0, 0), (1, 1), (0, 0), (0, 0)))


def reference(orbitals, offsets, pairs, live):
    def one(total, row):
        pair_row, alive = row
        first = pair_row[0]
        second = pair_row[1]
        shift = offsets[second] - offsets[first]
        own = orbitals[first]
        partner = place(orbitals[second], shift[0], shift[1])
        density = (own * partner)[None]
        potential = smooth(density, pad_first)[0]
        weight = alive.astype(jnp.float32)
        to_first = weight * potential * partner
        to_second = weight * place(potential * own, -shift[0], -shift[1])
        total = total.at[first].add(to_first)
        total = total.at[second].add(to_second)
        return total, None

    start = jnp.zeros(orbitals.shape, jnp.float32)
    result, _ = lax.scan(one, start, (pairs, live))
    return result
```

```python
import functools

import jax
import jax.numpy as jnp
from jax import lax
from jax.experimental import pallas as pl
from jax.experimental.pallas import tpu as pltpu
from jax.sharding import PartitionSpec as P

PASSES = 8
DIAG = 6.25
THETA = 1.075
DELTA = 0.925

BOX = 64
LANES = 128
PAD = 16
ROWS = BOX + 2 * PAD
VMEM_BYTES = 40 * 1024 * 1024


def params():
    return pltpu.CompilerParams(vmem_limit_bytes=VMEM_BYTES)


def shifted(shard, axis, by):
    size = lax.axis_size(axis)
    return lax.ppermute(shard, axis, [(i, (i + by) % size) for i in range(size)])


def lane_index(shape):
    return lax.broadcasted_iota(jnp.int32, shape, len(shape) - 1)


def moved_z(field, by):
    z = lane_index(field.shape) & (BOX - 1)
    source = z - by
    rolled = pltpu.roll(field, jnp.where(by < 0, by + LANES, by), 1)
    return jnp.where((source >= 0) & (source < BOX), rolled, 0.0)


def pack_kernel(field_ref, out_ref):
    half = field_ref.shape[1] // 2
    out_ref[...] = jnp.concatenate([field_ref[:, :half], field_ref[:, half:]], axis=-1)


def pack(orbitals):
    orbs, planes = orbitals.shape[:2]
    return pl.pallas_call(
        pack_kernel,
        grid=(2,),
        in_specs=[pl.BlockSpec((orbs // 2, planes, BOX, BOX), lambda i: (i, 0, 0, 0))],
        out_specs=pl.BlockSpec((orbs // 2, planes // 2, BOX, LANES), lambda i: (i, 0, 0, 0)),
        out_shape=jax.ShapeDtypeStruct((orbs, planes // 2, BOX, LANES), jnp.float32),
        compiler_params=params(),
    )(orbitals)


def finish_kernel(mid_ref, next_ref, prior_ref, out_ref):
    half = mid_ref.shape[1]
    total = mid_ref[...] + next_ref[...] + prior_ref[...]
    out_ref[:, :half] = total[..., :BOX]
    out_ref[:, half:] = total[..., BOX:]


def finish(middle, from_next, from_prior):
    orbs, half = middle.shape[:2]
    spec = pl.BlockSpec((orbs // 2, half, BOX, LANES), lambda i: (i, 0, 0, 0))
    return pl.pallas_call(
        finish_kernel,
        grid=(2,),
        in_specs=[spec] * 3,
        out_specs=pl.BlockSpec((orbs // 2, 2 * half, BOX, BOX), lambda i: (i, 0, 0, 0)),
        out_shape=jax.ShapeDtypeStruct((orbs, 2 * half, BOX, BOX), jnp.float32),
        compiler_params=params(),
    )(middle, from_next, from_prior)


def clear_pads(ext):
    zeros = jnp.zeros((ext.shape[1], PAD, LANES), jnp.float32)

    @pl.loop(0, ext.shape[0])
    def _(orb):
        ext[orb, :, :PAD] = zeros
        ext[orb, :, PAD + BOX :] = zeros


def fetch(refs, ext, sems):
    copies = []
    for k, ref in enumerate(refs):
        orbs = ref.shape[0]
        copies.append(
            pltpu.make_async_copy(
                ref, ext.at[pl.ds(k * orbs, orbs), :, pl.ds(PAD, BOX), :], sems.at[k]
            )
        )
    for copy in copies:
        copy.start()
    return copies


def density_kernel(table_ref, prev_ref, own_ref, next_ref, out_ref, ext, sems):
    copies = fetch((prev_ref, own_ref, next_ref), ext, sems)
    clear_pads(ext)
    for copy in copies:
        copy.wait()
    slots, planes = out_ref.shape[:2]

    @pl.loop(0, slots)
    def _(slot):
        first = table_ref[0, slot]
        second = table_ref[1, slot]
        by_y = table_ref[2, slot]
        by_z = table_ref[3, slot]
        for x in range(planes):
            partner = moved_z(ext[second, x, pl.ds(PAD - by_y, BOX), :], by_z)
            out_ref[slot, x] = ext[first, x, PAD : PAD + BOX, :] * partner


def densities(table, prev, own, after):
    slots = table.shape[1]
    orbs, planes = own.shape[:2]
    return pl.pallas_call(
        density_kernel,
        in_specs=[pl.BlockSpec(memory_space=pltpu.SMEM)] + [pl.BlockSpec(memory_space=pl.ANY)] * 3,
        out_specs=pl.BlockSpec(memory_space=pltpu.VMEM),
        out_shape=jax.ShapeDtypeStruct((slots, planes, BOX, LANES), jnp.float32),
        scratch_shapes=[
            pltpu.VMEM((3 * orbs, planes, ROWS, LANES), jnp.float32),
            pltpu.SemaphoreType.DMA((3,)),
        ],
        compiler_params=params(),
    )(table, prev, own, after)


def exchange_kernel(
    table_ref, pot_ref, prev_ref, own_ref, next_ref, before_ref, mid_ref, after_ref, ext, acc, moved, sems
):
    copies = fetch((prev_ref, own_ref, next_ref), ext, sems)
    clear_pads(ext)
    orbs, planes = mid_ref.shape[:2]
    zeros = jnp.zeros((planes, BOX, LANES), jnp.float32)

    @pl.loop(0, 3 * orbs)
    def _(orb):
        acc[orb] = zeros

    for x in range(planes):
        moved[x, :PAD] = jnp.zeros((PAD, LANES), jnp.float32)
        moved[x, PAD + BOX :] = jnp.zeros((PAD, LANES), jnp.float32)
    for copy in copies:
        copy.wait()

    @pl.loop(0, table_ref.shape[1])
    def _(slot):
        first = table_ref[0, slot]
        second = table_ref[1, slot]
        by_y = table_ref[2, slot]
        by_z = table_ref[3, slot]
        weight = table_ref[4, slot].astype(jnp.float32)
        for x in range(planes):
            pot = weight * pot_ref[slot, x]
            partner = moved_z(ext[second, x, pl.ds(PAD - by_y, BOX), :], by_z)
            acc[first, x] += pot * partner
            moved[x, PAD : PAD + BOX] = moved_z(pot * ext[first, x, PAD : PAD + BOX, :], -by_z)
        for x in range(planes):
            acc[second, x] += moved[x, pl.ds(PAD + by_y, BOX), :]

    before_ref[...] = acc[:orbs]
    mid_ref[...] = acc[orbs : 2 * orbs]
    after_ref[...] = acc[2 * orbs :]


def exchange_terms(table, potential, prev, own, after):
    orbs, planes = own.shape[:2]
    vmem = pl.BlockSpec(memory_space=pltpu.VMEM)
    return pl.pallas_call(
        exchange_kernel,
        in_specs=[pl.BlockSpec(memory_space=pltpu.SMEM), vmem] + [pl.BlockSpec(memory_space=pl.ANY)] * 3,
        out_specs=[vmem] * 3,
        out_shape=[jax.ShapeDtypeStruct(own.shape, jnp.float32)] * 3,
        scratch_shapes=[
            pltpu.VMEM((3 * orbs, planes, ROWS, LANES), jnp.float32),
            pltpu.VMEM((3 * orbs, planes, BOX, LANES), jnp.float32),
            pltpu.VMEM((planes, ROWS, LANES), jnp.float32),
            pltpu.SemaphoreType.DMA((3,)),
        ],
        compiler_params=params(),
    )(table, potential, prev, own, after)


EDGE = 8
HALF = BOX // 2


def coefficients():
    sigma = THETA / DELTA
    coef = 1.0 / sigma
    made = []
    for _ in range(PASSES - 1):
        new = 1.0 / (2.0 * sigma - coef)
        made.append((new * coef, 2.0 * new / (DELTA * DIAG)))
        coef = new
    return made


def solve_kernel(dens_ref, out_ref, resid, value, step_a, step_b):
    slabs, planes = dens_ref.shape[:2]
    lane = lane_index((BOX, LANES))
    low = lane < BOX
    z = lane & (BOX - 1)
    not_first = z > 0
    not_last = z < BOX - 1
    core = slice(EDGE, EDGE + BOX)

    for step in (step_a, step_b):

        @pl.loop(0, HALF + 2)
        def _(x):
            step[x, :EDGE] = jnp.zeros((EDGE, LANES), jnp.float32)
            step[x, EDGE + BOX :] = jnp.zeros((EDGE, LANES), jnp.float32)

    def seam(step):
        last = pltpu.roll(step[HALF, core, :], BOX, 1)
        step[0, core, :] = jnp.where(low, 0.0, last)
        leading = pltpu.roll(step[1, core, :], BOX, 1)
        step[HALF + 1, core, :] = jnp.where(low, leading, 0.0)

    @pl.loop(0, slabs // 2)
    def _(slab):
        for k in range(planes):
            one = dens_ref[slab, k]
            two = dens_ref[slab + slabs // 2, k]
            near = jnp.where(low, one, pltpu.roll(two, BOX, 1))
            far = jnp.where(low, pltpu.roll(one, BOX, 1), two)
            for x, plane in ((2 * planes * slab + k, near), (2 * planes * slab + planes + k, far)):
                start = plane * (1.0 / (DIAG * THETA))
                resid[x] = plane
                value[x] = start
                step_a[x + 1, core, :] = start

    seam(step_a)
    old, new = step_a, step_b
    for keep, add in coefficients():

        @pl.loop(0, HALF, unroll=2)
        def _(x):
            mid = old[x + 1, core, :]
            near = old[x, core, :] + old[x + 2, core, :]
            near = near + old[x + 1, EDGE - 1 : EDGE - 1 + BOX, :]
            near = near + old[x + 1, EDGE + 1 : EDGE + 1 + BOX, :]
            near = near + jnp.where(not_first, pltpu.roll(mid, 1, 1), 0.0)
            near = near + jnp.where(not_last, pltpu.roll(mid, LANES - 1, 1), 0.0)
            left = (resid[x] - DIAG * mid) + near
            resid[x] = left
            fresh = keep * mid + add * left
            new[x + 1, core, :] = fresh
            value[x] += fresh

        seam(new)
        old, new = new, old

    @pl.loop(0, slabs // 2)
    def _(slab):
        for k in range(planes):
            near = value[2 * planes * slab + k]
            far = value[2 * planes * slab + planes + k]
            out_ref[slab, k] = jnp.where(low, near, pltpu.roll(far, BOX, 1))
            out_ref[slab + slabs // 2, k] = jnp.where(low, pltpu.roll(near, BOX, 1), far)


def solve(density):
    vmem = pl.BlockSpec(memory_space=pltpu.VMEM)
    return pl.pallas_call(
        solve_kernel,
        in_specs=[vmem],
        out_specs=vmem,
        out_shape=jax.ShapeDtypeStruct(density.shape, jnp.float32),
        scratch_shapes=[
            pltpu.VMEM((HALF, BOX, LANES), jnp.float32),
            pltpu.VMEM((HALF, BOX, LANES), jnp.float32),
            pltpu.VMEM((HALF + 2, BOX + 2 * EDGE, LANES), jnp.float32),
            pltpu.VMEM((HALF + 2, BOX + 2 * EDGE, LANES), jnp.float32),
        ],
        compiler_params=params(),
    )(density)


def slot_table(offsets, pairs, live, orb_dev):
    total_orbs = offsets.shape[0]
    start = lax.axis_index(("grp", "orb")) * orb_dev - orb_dev
    local = jnp.mod(pairs - start, total_orbs)
    ids = jnp.arange(total_orbs, dtype=jnp.int32)
    pick_first = (pairs[:, 0:1] == ids[None, :]).astype(jnp.int32)
    pick_second = (pairs[:, 1:2] == ids[None, :]).astype(jnp.int32)
    shift = jnp.sum((pick_second - pick_first)[:, :, None] * offsets[None, :, :], axis=1)
    return jnp.concatenate([local.T, shift.T, live[None, :]], axis=0)


def swap(slabs):
    return lax.all_to_all(slabs, "slab", split_axis=0, concat_axis=0, tiled=True)


def body(orbitals, offsets, pairs, live):
    ring = ("grp", "orb")
    table = slot_table(offsets, pairs, live, orbitals.shape[0])
    own = pack(orbitals)
    prev = shifted(own, ring, 1)
    after = shifted(own, ring, -1)
    potential = swap(solve(swap(densities(table, prev, own, after))))
    to_prior, middle, to_next = exchange_terms(table, potential, prev, own, after)
    return finish(middle, shifted(to_prior, ring, -1), shifted(to_next, ring, 1))


def solution(mesh):
    placed = (
        P(("grp", "orb"), "slab", None, None),
        P(),
        P(("grp", "orb"), None),
        P(("grp", "orb")),
    )
    return jax.shard_map(
        body,
        mesh=mesh,
        in_specs=placed,
        out_specs=P(("grp", "orb"), "slab", None, None),
        check_vma=False,
    )
```

```python
import functools

import jax
import jax.numpy as jnp
from jax import lax
from jax.experimental import pallas as pl
from jax.experimental.pallas import tpu as pltpu
from jax.sharding import PartitionSpec as P

PASSES = 8
DIAG = 6.25
THETA = 1.075
DELTA = 0.925

BOX = 64
LANES = 128
PAD = 16
ROWS = BOX + 2 * PAD
VMEM_BYTES = 40 * 1024 * 1024


def params():
    return pltpu.CompilerParams(vmem_limit_bytes=VMEM_BYTES)


def shifted(shard, axis, by):
    size = lax.axis_size(axis)
    return lax.ppermute(shard, axis, [(i, (i + by) % size) for i in range(size)])


def lane_index(shape):
    return lax.broadcasted_iota(jnp.int32, shape, len(shape) - 1)


def moved_z(field, by):
    z = lane_index(field.shape) & (BOX - 1)
    source = z - by
    rolled = pltpu.roll(field, jnp.where(by < 0, by + LANES, by), 1)
    return jnp.where((source >= 0) & (source < BOX), rolled, 0.0)


def pack_kernel(field_ref, out_ref):
    half = field_ref.shape[1] // 2
    out_ref[...] = jnp.concatenate([field_ref[:, :half], field_ref[:, half:]], axis=-1)


def pack(orbitals):
    orbs, planes = orbitals.shape[:2]
    return pl.pallas_call(
        pack_kernel,
        grid=(2,),
        in_specs=[pl.BlockSpec((orbs // 2, planes, BOX, BOX), lambda i: (i, 0, 0, 0))],
        out_specs=pl.BlockSpec((orbs // 2, planes // 2, BOX, LANES), lambda i: (i, 0, 0, 0)),
        out_shape=jax.ShapeDtypeStruct((orbs, planes // 2, BOX, LANES), jnp.float32),
        compiler_params=params(),
    )(orbitals)


def finish_kernel(mid_ref, next_ref, prior_ref, out_ref):
    half = mid_ref.shape[1]
    total = mid_ref[...] + next_ref[...] + prior_ref[...]
    out_ref[:, :half] = total[..., :BOX]
    out_ref[:, half:] = total[..., BOX:]


def finish(middle, from_next, from_prior):
    orbs, half = middle.shape[:2]
    spec = pl.BlockSpec((orbs // 2, half, BOX, LANES), lambda i: (i, 0, 0, 0))
    return pl.pallas_call(
        finish_kernel,
        grid=(2,),
        in_specs=[spec] * 3,
        out_specs=pl.BlockSpec((orbs // 2, 2 * half, BOX, BOX), lambda i: (i, 0, 0, 0)),
        out_shape=jax.ShapeDtypeStruct((orbs, 2 * half, BOX, BOX), jnp.float32),
        compiler_params=params(),
    )(middle, from_next, from_prior)


FIRST, SECOND, BY_Y, BY_Z, LIVE, SLAB = range(6)


def clear_pads(ext):
    zeros = jnp.zeros((ext.shape[1], PAD, LANES), jnp.float32)

    @pl.loop(0, ext.shape[0])
    def _(orb):
        ext[orb, :, :PAD] = zeros
        ext[orb, :, PAD + BOX :] = zeros


def fetch(refs, ext, sems):
    copies = []
    for k, ref in enumerate(refs):
        orbs = ref.shape[0]
        copies.append(
            pltpu.make_async_copy(
                ref, ext.at[pl.ds(k * orbs, orbs), :, pl.ds(PAD, BOX), :], sems.at[k]
            )
        )
    for copy in copies:
        copy.start()
    return copies


def swapped(field):
    return pltpu.roll(field, LANES // 2, 1)


def density_kernel(table_ref, prev_ref, own_ref, next_ref, *rest):
    out_refs, ext, sems = rest[:-2], rest[-2], rest[-1]
    copies = fetch((prev_ref, own_ref, next_ref), ext, sems)
    clear_pads(ext)
    for copy in copies:
        copy.wait()
    planes = own_ref.shape[1]
    low = lane_index((BOX, LANES)) < BOX

    def density(slot, x):
        first = table_ref[FIRST, slot]
        second = table_ref[SECOND, slot]
        partner = ext[second, x, pl.ds(PAD - table_ref[BY_Y, slot], BOX), :]
        return ext[first, x, PAD : PAD + BOX, :] * moved_z(partner, table_ref[BY_Z, slot])

    done = 0
    for out_ref in out_refs:
        count = out_ref.shape[0]

        @pl.loop(0, count)
        def _(pair):
            slot = 2 * (done + pair)
            for x in range(planes):
                one = density(slot, x)
                two = density(slot + 1, x)
                out_ref[pair, x] = jnp.where(low, one, swapped(two))
                out_ref[pair, planes + x] = jnp.where(low, swapped(one), two)

        done += count


def densities(table, prev, own, after, chunks):
    orbs, planes = own.shape[:2]
    return pl.pallas_call(
        density_kernel,
        in_specs=[pl.BlockSpec(memory_space=pltpu.SMEM)] + [pl.BlockSpec(memory_space=pl.ANY)] * 3,
        out_specs=[pl.BlockSpec(memory_space=pltpu.VMEM)] * len(chunks),
        out_shape=[
            jax.ShapeDtypeStruct((count, 2 * planes, BOX, LANES), jnp.float32) for count in chunks
        ],
        scratch_shapes=[
            pltpu.VMEM((3 * orbs, planes, ROWS, LANES), jnp.float32),
            pltpu.SemaphoreType.DMA((3,)),
        ],
        compiler_params=params(),
    )(table, prev, own, after)


def exchange_kernel(table_ref, prev_ref, own_ref, next_ref, *rest):
    pot_refs = rest[:-7]
    before_ref, mid_ref, after_ref, ext, acc, moved, sems = rest[-7:]
    copies = fetch((prev_ref, own_ref, next_ref), ext, sems)
    clear_pads(ext)
    orbs, planes = mid_ref.shape[:2]
    zeros = jnp.zeros((planes, BOX, LANES), jnp.float32)
    low = lane_index((BOX, LANES)) < BOX

    @pl.loop(0, 3 * orbs)
    def _(orb):
        acc[orb] = zeros

    for x in range(planes):
        moved[x, :PAD] = jnp.zeros((PAD, LANES), jnp.float32)
        moved[x, PAD + BOX :] = jnp.zeros((PAD, LANES), jnp.float32)
    for copy in copies:
        copy.wait()

    def add_terms(slot, potential):
        first = table_ref[FIRST, slot]
        second = table_ref[SECOND, slot]
        by_y = table_ref[BY_Y, slot]
        by_z = table_ref[BY_Z, slot]
        weight = table_ref[LIVE, slot].astype(jnp.float32)
        for x in range(planes):
            pot = weight * potential(x)
            partner = moved_z(ext[second, x, pl.ds(PAD - by_y, BOX), :], by_z)
            acc[first, x] += pot * partner
            moved[x, PAD : PAD + BOX] = moved_z(pot * ext[first, x, PAD : PAD + BOX, :], -by_z)
        for x in range(planes):
            acc[second, x] += moved[x, pl.ds(PAD + by_y, BOX), :]

    done = 0
    for pot_ref in pot_refs:
        count = pot_ref.shape[0]

        @pl.loop(0, count)
        def _(pair):
            slot = 2 * (done + pair)
            add_terms(
                slot,
                lambda x: jnp.where(low, pot_ref[pair, x], swapped(pot_ref[pair, planes + x])),
            )
            add_terms(
                slot + 1,
                lambda x: jnp.where(low, swapped(pot_ref[pair, x]), pot_ref[pair, planes + x]),
            )

        done += count

    before_ref[...] = acc[:orbs]
    mid_ref[...] = acc[orbs : 2 * orbs]
    after_ref[...] = acc[2 * orbs :]


def exchange_terms(table, potentials, prev, own, after):
    orbs, planes = own.shape[:2]
    vmem = pl.BlockSpec(memory_space=pltpu.VMEM)
    return pl.pallas_call(
        exchange_kernel,
        in_specs=[pl.BlockSpec(memory_space=pltpu.SMEM)]
        + [pl.BlockSpec(memory_space=pl.ANY)] * 3
        + [vmem] * len(potentials),
        out_specs=[vmem] * 3,
        out_shape=[jax.ShapeDtypeStruct(own.shape, jnp.float32)] * 3,
        scratch_shapes=[
            pltpu.VMEM((3 * orbs, planes, ROWS, LANES), jnp.float32),
            pltpu.VMEM((3 * orbs, planes, BOX, LANES), jnp.float32),
            pltpu.VMEM((planes, ROWS, LANES), jnp.float32),
            pltpu.SemaphoreType.DMA((3,)),
        ],
        compiler_params=params(),
    )(table, prev, own, after, *potentials)


SUB = 8


def coefficients():
    sigma = THETA / DELTA
    coef = 1.0 / sigma
    made = []
    for _ in range(PASSES - 1):
        new = 1.0 / (2.0 * sigma - coef)
        made.append((new * coef, 2.0 * new / (DELTA * DIAG)))
        coef = new
    return made


def solve_kernel(slabs, table_ref, far_ref, own_ref, near_ref, out_ref, dens, even, odd):
    slab = table_ref[SLAB, 0]
    pairs, planes = own_ref.shape[:2]
    flip = lax.rem(slab, 2)
    far_at = flip * 2 * planes
    near_at = (1 - flip) * 2 * planes
    z = lane_index((SUB, SUB, LANES)) & (BOX - 1)
    not_first = z > 0
    not_last = z < BOX - 1
    row = lax.broadcasted_iota(jnp.int32, (SUB, LANES), 0)
    below_in = jnp.where(slab > 0, 1.0, 0.0)
    above_in = jnp.where(slab < slabs - 1, 1.0, 0.0)
    core = slice(1, 1 + SUB)

    def put(buf, x, block):
        buf[x, core] = block
        buf[x, 0] = jnp.where(row > 0, pltpu.roll(block[SUB - 1], 1, 0), 0.0)
        buf[x, 1 + SUB] = jnp.where(row < SUB - 1, pltpu.roll(block[0], SUB - 1, 0), 0.0)

    def take(ref, pair, x):
        return jnp.stack([ref[pair, x, pl.ds(t, SUB, stride=SUB), :] for t in range(SUB)])

    @pl.loop(0, pairs)
    def _(pair):
        for x in range(planes):
            put(dens, far_at + x, take(far_ref, pair, x))
            put(dens, planes + x, take(own_ref, pair, x))
            put(dens, near_at + x, take(near_ref, pair, x))
        start = 1.0 / (DIAG * THETA)
        for turn, (keep, add) in enumerate(coefficients(), 1):
            source = dens if turn == 1 else (even if turn % 2 else odd)
            target = odd if turn % 2 else even
            here = 1.0 + keep - DIAG * add
            for x in range(turn + 1, 3 * planes - 1 - turn):
                mid = source[x, core]
                near = source[x - 1, core] + source[x + 1, core]
                near = near + (source[x, :SUB] + source[x, 2 : 2 + SUB])
                near = near + jnp.where(not_first, pltpu.roll(mid, 1, 2), 0.0)
                near = near + jnp.where(not_last, pltpu.roll(mid, LANES - 1, 2), 0.0)
                if turn == 1:
                    fresh = (here * start + add) * mid + (add * start) * near
                elif turn == 2:
                    fresh = here * mid + (add - keep * start) * dens[x, core] + add * near
                else:
                    fresh = here * mid - keep * target[x, core] + add * (near + dens[x, core])
                if x < planes:
                    fresh = fresh * below_in
                if x >= 2 * planes:
                    fresh = fresh * above_in
                if turn < PASSES - 1:
                    put(target, x, fresh)
                else:
                    for t in range(SUB):
                        out_ref[pair, x - planes, pl.ds(t, SUB, stride=SUB), :] = fresh[t]


def solve(table, far, own, near, slabs):
    planes = own.shape[1]
    vmem = pl.BlockSpec(memory_space=pltpu.VMEM)
    return pl.pallas_call(
        functools.partial(solve_kernel, slabs),
        in_specs=[pl.BlockSpec(memory_space=pltpu.SMEM), vmem, vmem, vmem],
        out_specs=vmem,
        out_shape=jax.ShapeDtypeStruct(own.shape, jnp.float32),
        scratch_shapes=[pltpu.VMEM((3 * planes, SUB + 2, SUB, LANES), jnp.float32)] * 3,
        compiler_params=params(),
    )(table, far, own, near)


def slot_table(offsets, pairs, live, orb_dev):
    total_orbs = offsets.shape[0]
    start = lax.axis_index(("grp", "orb")) * orb_dev - orb_dev
    local = jnp.mod(pairs - start, total_orbs)
    ids = jnp.arange(total_orbs, dtype=jnp.int32)
    pick_first = (pairs[:, 0:1] == ids[None, :]).astype(jnp.int32)
    pick_second = (pairs[:, 1:2] == ids[None, :]).astype(jnp.int32)
    shift = jnp.sum((pick_second - pick_first)[:, :, None] * offsets[None, :, :], axis=1)
    slab = jnp.broadcast_to(lax.axis_index("slab").astype(jnp.int32), (1, pairs.shape[0]))
    return jnp.concatenate([local.T, shift.T, live[None, :], slab], axis=0)


def solved_terms(count, table, prev, own, after):
    slabs = lax.axis_size("slab")
    across = [(s, s ^ 1) for s in range(slabs)]
    onward = [(s, s + 2 - 4 * (s % 2)) for s in range(slabs)]
    onward = [(s, t) for s, t in onward if 0 <= t < slabs]
    chunks = [count] if count == 1 else [count - count // 2, count // 2]
    made = densities(table, prev, own, after, chunks)
    near = [lax.ppermute(dens, "slab", across) for dens in made]
    far = [lax.ppermute(dens, "slab", onward) for dens in near]
    potentials = [solve(table, f, d, n, slabs) for f, d, n in zip(far, made, near)]
    return exchange_terms(table, potentials, prev, own, after)


def body(orbitals, offsets, pairs, live):
    ring = ("grp", "orb")
    table = slot_table(offsets, pairs, live, orbitals.shape[0])
    own = pack(orbitals)
    prev = shifted(own, ring, 1)
    after = shifted(own, ring, -1)
    most = (live.shape[0] + 1) // 2
    count = jnp.clip((jnp.sum(live) + 1) // 2, 1, most)
    to_prior, middle, to_next = lax.switch(
        count - 1,
        [functools.partial(solved_terms, k) for k in range(1, most + 1)],
        table,
        prev,
        own,
        after,
    )
    return finish(middle, shifted(to_prior, ring, -1), shifted(to_next, ring, 1))


def solution(mesh):
    placed = (
        P(("grp", "orb"), "slab", None, None),
        P(),
        P(("grp", "orb"), None),
        P(("grp", "orb")),
    )
    return jax.shard_map(
        body,
        mesh=mesh,
        in_specs=placed,
        out_specs=P(("grp", "orb"), "slab", None, None),
        check_vma=False,
    )
```

```python
import functools

import jax
import jax.numpy as jnp
from jax import lax
from jax.experimental import pallas as pl
from jax.experimental.pallas import tpu as pltpu
from jax.sharding import PartitionSpec as P

PASSES = 8
DIAG = 6.25
THETA = 1.075
DELTA = 0.925

BOX = 64
LANES = 128
PAD = 16
ROWS = BOX + 2 * PAD
VMEM_BYTES = 40 * 1024 * 1024


def params():
    return pltpu.CompilerParams(vmem_limit_bytes=VMEM_BYTES)


RING = ("grp", "orb")


def even_edges():
    return [(g, g ^ 1) for g in range(lax.axis_size(RING))]


def odd_edges():
    size = lax.axis_size(RING)
    return [(g, (g + 1 if g % 2 else g - 1) % size) for g in range(size)]


def lane_index(shape):
    return lax.broadcasted_iota(jnp.int32, shape, len(shape) - 1)


def moved_z(field, by):
    z = lane_index(field.shape) & (BOX - 1)
    source = z - by
    rolled = pltpu.roll(field, jnp.where(by < 0, by + LANES, by), 1)
    return jnp.where((source >= 0) & (source < BOX), rolled, 0.0)


def pack_kernel(field_ref, out_ref):
    half = field_ref.shape[1] // 2
    out_ref[...] = jnp.concatenate([field_ref[:, :half], field_ref[:, half:]], axis=-1)


def pack(orbitals):
    orbs, planes = orbitals.shape[:2]
    return pl.pallas_call(
        pack_kernel,
        grid=(2,),
        in_specs=[pl.BlockSpec((orbs // 2, planes, BOX, BOX), lambda i: (i, 0, 0, 0))],
        out_specs=pl.BlockSpec((orbs // 2, planes // 2, BOX, LANES), lambda i: (i, 0, 0, 0)),
        out_shape=jax.ShapeDtypeStruct((orbs, planes // 2, BOX, LANES), jnp.float32),
        compiler_params=params(),
    )(orbitals)


def finish_kernel(table_ref, asked_ref, mid_ref, pal_ref, far_ref, out_ref, acc):
    orbs, half = mid_ref.shape[:2]
    acc[...] = mid_ref[...] + pal_ref[...]
    rank = 0
    for slot in range(asked_ref.shape[0]):
        local = asked_ref[slot] - orbs * table_ref[GROUP, 0]
        hit = (local >= 0) & (local < orbs)
        if slot:
            rank = jnp.minimum(rank, far_ref.shape[0] - 1)

        @pl.when(hit)
        def _():
            acc[local] += far_ref[rank]

        rank += hit.astype(jnp.int32)
    out_ref[:, :half] = acc[..., :BOX]
    out_ref[:, half:] = acc[..., BOX:]


def finish(table, asked, middle, from_pal, from_far):
    orbs, half = middle.shape[:2]
    smem = pl.BlockSpec(memory_space=pltpu.SMEM)
    vmem = pl.BlockSpec(memory_space=pltpu.VMEM)
    return pl.pallas_call(
        finish_kernel,
        in_specs=[smem, smem, vmem, vmem, vmem],
        out_specs=vmem,
        out_shape=jax.ShapeDtypeStruct((orbs, 2 * half, BOX, BOX), jnp.float32),
        scratch_shapes=[pltpu.VMEM(middle.shape, jnp.float32)],
        compiler_params=params(),
    )(table, asked, middle, from_pal, from_far)


def gather_kernel(table_ref, asked_ref, own_ref, out_ref, sems):
    orbs, count = own_ref.shape[0], out_ref.shape[0]
    chosen = [0] * count
    rank = 0
    for slot in range(asked_ref.shape[0]):
        local = asked_ref[slot] - orbs * table_ref[GROUP, 0]
        hit = (local >= 0) & (local < orbs)
        chosen = [jnp.where(hit & (rank == k), local, old) for k, old in enumerate(chosen)]
        rank += hit.astype(jnp.int32)
    copies = [
        pltpu.make_async_copy(own_ref.at[orb], out_ref.at[k], sems.at[k])
        for k, orb in enumerate(chosen)
    ]
    for copy in copies:
        copy.start()
    for copy in copies:
        copy.wait()


def gather(table, asked, own, count):
    smem = pl.BlockSpec(memory_space=pltpu.SMEM)
    anywhere = pl.BlockSpec(memory_space=pl.ANY)
    return pl.pallas_call(
        gather_kernel,
        in_specs=[smem, smem, anywhere],
        out_specs=anywhere,
        out_shape=jax.ShapeDtypeStruct((count,) + own.shape[1:], jnp.float32),
        scratch_shapes=[pltpu.SemaphoreType.DMA((count,))],
        compiler_params=params(),
    )(table, asked, own)


def spread_kernel(in_ref, out_ref, sem):
    copy = pltpu.make_async_copy(in_ref, out_ref.at[pl.ds(0, in_ref.shape[0])], sem)
    copy.start()
    copy.wait()


def spread(blocks, count):
    if blocks.shape[0] == count:
        return blocks
    anywhere = pl.BlockSpec(memory_space=pl.ANY)
    return pl.pallas_call(
        spread_kernel,
        in_specs=[anywhere],
        out_specs=anywhere,
        out_shape=jax.ShapeDtypeStruct((count,) + blocks.shape[1:], jnp.float32),
        scratch_shapes=[pltpu.SemaphoreType.DMA],
        compiler_params=params(),
    )(blocks)


def ask(count, most, table, asked, own):
    return spread(lax.ppermute(gather(table, asked, own, count), RING, odd_edges()), most)


def answer(count, most, terms):
    return spread(lax.ppermute(terms[:count], RING, odd_edges()), most)


FIRST, SECOND, BY_Y, BY_Z, GROUP, SLAB = range(6)


def locate(table_ref, where_ref, orbs):
    group = table_ref[GROUP, 0]
    pal = group ^ 1
    rank = 0
    for slot in range(where_ref.shape[0]):
        second = table_ref[SECOND, slot]
        mine = second - orbs * group
        other = second - orbs * pal
        is_mine = (mine >= 0) & (mine < orbs)
        is_pal = (other >= 0) & (other < orbs)
        is_far = (second >= 0) & ~is_mine & ~is_pal
        place = jnp.where(is_pal, orbs + other, jnp.where(is_far, 2 * orbs + rank, 0))
        where_ref[slot] = jnp.where(is_mine, mine, place)
        rank += is_far.astype(jnp.int32)


def clear_pads(ext):
    zeros = jnp.zeros((ext.shape[1], PAD, LANES), jnp.float32)

    @pl.loop(0, ext.shape[0])
    def _(orb):
        ext[orb, :, :PAD] = zeros
        ext[orb, :, PAD + BOX :] = zeros


def fetch(refs, ext, sems):
    copies = []
    done = 0
    for k, ref in enumerate(refs):
        orbs = ref.shape[0]
        target = ext.at[pl.ds(done, orbs), :, pl.ds(PAD, BOX), :]
        copies.append(pltpu.make_async_copy(ref, target, sems.at[k]))
        done += orbs
    for copy in copies:
        copy.start()
    return copies


def swapped(field):
    return pltpu.roll(field, LANES // 2, 1)


def density_kernel(table_ref, own_ref, pal_ref, far_ref, *rest):
    out_refs, (ext, where, sems) = rest[:-3], rest[-3:]
    copies = fetch((own_ref, pal_ref, far_ref), ext, sems)
    clear_pads(ext)
    locate(table_ref, where, own_ref.shape[0])
    for copy in copies:
        copy.wait()
    planes = own_ref.shape[1]
    low = lane_index((BOX, LANES)) < BOX

    def density(slot, x):
        first = table_ref[FIRST, slot]
        second = where[slot]
        partner = ext[second, x, pl.ds(PAD - table_ref[BY_Y, slot], BOX), :]
        return ext[first, x, PAD : PAD + BOX, :] * moved_z(partner, table_ref[BY_Z, slot])

    done = 0
    for out_ref in out_refs:
        count = out_ref.shape[0]

        @pl.loop(0, count)
        def _(pair):
            slot = 2 * (done + pair)
            for x in range(planes):
                one = density(slot, x)
                two = density(slot + 1, x)
                out_ref[pair, x] = jnp.where(low, one, swapped(two))
                out_ref[pair, planes + x] = jnp.where(low, swapped(one), two)

        done += count


def densities(table, own, pal, far, chunks):
    orbs, planes = own.shape[:2]
    return pl.pallas_call(
        density_kernel,
        in_specs=[pl.BlockSpec(memory_space=pltpu.SMEM)] + [pl.BlockSpec(memory_space=pl.ANY)] * 3,
        out_specs=[pl.BlockSpec(memory_space=pltpu.VMEM)] * len(chunks),
        out_shape=[
            jax.ShapeDtypeStruct((count, 2 * planes, BOX, LANES), jnp.float32) for count in chunks
        ],
        scratch_shapes=[
            pltpu.VMEM((2 * orbs + far.shape[0], planes, ROWS, LANES), jnp.float32),
            pltpu.SMEM((table.shape[1],), jnp.int32),
            pltpu.SemaphoreType.DMA((3,)),
        ],
        compiler_params=params(),
    )(table, own, pal, far)


def exchange_kernel(table_ref, own_ref, pal_ref, far_ref, *rest):
    pot_refs = rest[:-8]
    mid_ref, to_pal_ref, to_far_ref, ext, acc, moved, where, sems = rest[-8:]
    copies = fetch((own_ref, pal_ref, far_ref), ext, sems)
    clear_pads(ext)
    locate(table_ref, where, own_ref.shape[0])
    orbs, planes = mid_ref.shape[:2]
    zeros = jnp.zeros((planes, BOX, LANES), jnp.float32)
    low = lane_index((BOX, LANES)) < BOX

    @pl.loop(0, acc.shape[0])
    def _(orb):
        acc[orb] = zeros

    for x in range(planes):
        moved[x, :PAD] = jnp.zeros((PAD, LANES), jnp.float32)
        moved[x, PAD + BOX :] = jnp.zeros((PAD, LANES), jnp.float32)
    for copy in copies:
        copy.wait()

    def add_terms(slot, potential):
        first = table_ref[FIRST, slot]
        second = where[slot]
        by_y = table_ref[BY_Y, slot]
        by_z = table_ref[BY_Z, slot]
        weight = jnp.where(table_ref[SECOND, slot] >= 0, 1.0, 0.0)
        for x in range(planes):
            pot = weight * potential(x)
            partner = moved_z(ext[second, x, pl.ds(PAD - by_y, BOX), :], by_z)
            acc[first, x] += pot * partner
            moved[x, PAD : PAD + BOX] = moved_z(pot * ext[first, x, PAD : PAD + BOX, :], -by_z)
        for x in range(planes):
            acc[second, x] += moved[x, pl.ds(PAD + by_y, BOX), :]

    done = 0
    for pot_ref in pot_refs:
        count = pot_ref.shape[0]

        @pl.loop(0, count)
        def _(pair):
            slot = 2 * (done + pair)
            add_terms(
                slot,
                lambda x: jnp.where(low, pot_ref[pair, x], swapped(pot_ref[pair, planes + x])),
            )
            add_terms(
                slot + 1,
                lambda x: jnp.where(low, swapped(pot_ref[pair, x]), pot_ref[pair, planes + x]),
            )

        done += count

    mid_ref[...] = acc[:orbs]
    to_pal_ref[...] = acc[orbs : 2 * orbs]
    to_far_ref[...] = acc[2 * orbs :]


def exchange_terms(table, potentials, own, pal, far):
    orbs, planes = own.shape[:2]
    vmem = pl.BlockSpec(memory_space=pltpu.VMEM)
    return pl.pallas_call(
        exchange_kernel,
        in_specs=[pl.BlockSpec(memory_space=pltpu.SMEM)]
        + [pl.BlockSpec(memory_space=pl.ANY)] * 3
        + [vmem] * len(potentials),
        out_specs=[vmem] * 3,
        out_shape=[jax.ShapeDtypeStruct(a.shape, jnp.float32) for a in (own, pal, far)],
        scratch_shapes=[
            pltpu.VMEM((2 * orbs + far.shape[0], planes, ROWS, LANES), jnp.float32),
            pltpu.VMEM((2 * orbs + far.shape[0], planes, BOX, LANES), jnp.float32),
            pltpu.VMEM((planes, ROWS, LANES), jnp.float32),
            pltpu.SMEM((table.shape[1],), jnp.int32),
            pltpu.SemaphoreType.DMA((3,)),
        ],
        compiler_params=params(),
    )(table, own, pal, far, *potentials)


SUB = 8


def coefficients():
    sigma = THETA / DELTA
    coef = 1.0 / sigma
    made = []
    for _ in range(PASSES - 1):
        new = 1.0 / (2.0 * sigma - coef)
        made.append((new * coef, 2.0 * new / (DELTA * DIAG)))
        coef = new
    return made


def solve_kernel(slabs, table_ref, far_ref, own_ref, near_ref, out_ref, dens, even, odd):
    slab = table_ref[SLAB, 0]
    pairs, planes = own_ref.shape[:2]
    flip = lax.rem(slab, 2)
    far_at = flip * 2 * planes
    near_at = (1 - flip) * 2 * planes
    z = lane_index((SUB, SUB, LANES)) & (BOX - 1)
    not_first = z > 0
    not_last = z < BOX - 1
    row = lax.broadcasted_iota(jnp.int32, (SUB, LANES), 0)
    below_in = jnp.where(slab > 0, 1.0, 0.0)
    above_in = jnp.where(slab < slabs - 1, 1.0, 0.0)
    core = slice(1, 1 + SUB)

    def put(buf, x, block):
        buf[x, core] = block
        buf[x, 0] = jnp.where(row > 0, pltpu.roll(block[SUB - 1], 1, 0), 0.0)
        buf[x, 1 + SUB] = jnp.where(row < SUB - 1, pltpu.roll(block[0], SUB - 1, 0), 0.0)

    def take(ref, pair, x):
        return jnp.stack([ref[pair, x, pl.ds(t, SUB, stride=SUB), :] for t in range(SUB)])

    @pl.loop(0, pairs)
    def _(pair):
        for x in range(planes):
            put(dens, far_at + x, take(far_ref, pair, x))
            put(dens, planes + x, take(own_ref, pair, x))
            put(dens, near_at + x, take(near_ref, pair, x))
        start = 1.0 / (DIAG * THETA)
        for turn, (keep, add) in enumerate(coefficients(), 1):
            source = dens if turn == 1 else (even if turn % 2 else odd)
            target = odd if turn % 2 else even
            here = 1.0 + keep - DIAG * add
            for x in range(turn + 1, 3 * planes - 1 - turn):
                mid = source[x, core]
                near = source[x - 1, core] + source[x + 1, core]
                near = near + (source[x, :SUB] + source[x, 2 : 2 + SUB])
                near = near + jnp.where(not_first, pltpu.roll(mid, 1, 2), 0.0)
                near = near + jnp.where(not_last, pltpu.roll(mid, LANES - 1, 2), 0.0)
                if turn == 1:
                    fresh = (here * start + add) * mid + (add * start) * near
                elif turn == 2:
                    fresh = here * mid + (add - keep * start) * dens[x, core] + add * near
                else:
                    fresh = here * mid - keep * target[x, core] + add * (near + dens[x, core])
                if x < planes:
                    fresh = fresh * below_in
                if x >= 2 * planes:
                    fresh = fresh * above_in
                if turn < PASSES - 1:
                    put(target, x, fresh)
                else:
                    for t in range(SUB):
                        out_ref[pair, x - planes, pl.ds(t, SUB, stride=SUB), :] = fresh[t]


def solve(table, far, own, near, slabs):
    planes = own.shape[1]
    vmem = pl.BlockSpec(memory_space=pltpu.VMEM)
    return pl.pallas_call(
        functools.partial(solve_kernel, slabs),
        in_specs=[pl.BlockSpec(memory_space=pltpu.SMEM), vmem, vmem, vmem],
        out_specs=vmem,
        out_shape=jax.ShapeDtypeStruct(own.shape, jnp.float32),
        scratch_shapes=[pltpu.VMEM((3 * planes, SUB + 2, SUB, LANES), jnp.float32)] * 3,
        compiler_params=params(),
    )(table, far, own, near)


def slot_table(offsets, pairs, seconds, orb_dev):
    total_orbs = offsets.shape[0]
    group = lax.axis_index(RING).astype(jnp.int32)
    ids = jnp.arange(total_orbs, dtype=jnp.int32)
    pick_first = (pairs[:, 0:1] == ids[None, :]).astype(jnp.int32)
    pick_second = (pairs[:, 1:2] == ids[None, :]).astype(jnp.int32)
    shift = jnp.sum((pick_second - pick_first)[:, :, None] * offsets[None, :, :], axis=1)
    constants = jnp.stack([group, lax.axis_index("slab").astype(jnp.int32)])
    return jnp.concatenate(
        [
            (pairs[:, 0] - orb_dev * group)[None, :],
            seconds[None, :],
            shift.T,
            jnp.broadcast_to(constants[:, None], (2, pairs.shape[0])),
        ],
        axis=0,
    )


def asked_by(seconds, group, orb_dev):
    local = seconds - orb_dev * group
    return jnp.sum(((local >= 0) & (local < orb_dev)).astype(jnp.int32))


def solved_terms(count, table, own, pal, far):
    slabs = lax.axis_size("slab")
    across = [(s, s ^ 1) for s in range(slabs)]
    onward = [(s, s + 2 - 4 * (s % 2)) for s in range(slabs)]
    onward = [(s, t) for s, t in onward if 0 <= t < slabs]
    chunks = [count] if count == 1 else [count - count // 2, count // 2]
    made = densities(table, own, pal, far, chunks)
    near = [lax.ppermute(dens, "slab", across) for dens in made]
    next_but_one = [lax.ppermute(dens, "slab", onward) for dens in near]
    potentials = [solve(table, f, d, n, slabs) for f, d, n in zip(next_but_one, made, near)]
    return exchange_terms(table, potentials, own, pal, far)


def body(orbitals, offsets, pairs, live):
    orbs, slots = orbitals.shape[0], live.shape[0]
    seconds = jnp.where(live > 0, pairs[:, 1], -1)
    asked = lax.ppermute(seconds, RING, odd_edges())
    own = pack(orbitals)
    pal = lax.ppermute(own, RING, even_edges())
    table = slot_table(offsets, pairs, seconds, orbs)

    group = lax.axis_index(RING)
    beyond = (group + 2 * (group % 2) - 1) % lax.axis_size(RING)
    most = slots - 1
    longer = jnp.maximum(asked_by(asked, group, orbs), asked_by(seconds, beyond, orbs))
    length = jnp.clip(longer, 1, most) - 1
    lengths = range(1, most + 1)
    asks = [functools.partial(ask, k, most) for k in lengths]
    far = lax.switch(length, asks, table, asked, own)

    pairs_most = (slots + 1) // 2
    count = jnp.clip((jnp.sum(live) + 1) // 2, 1, pairs_most)
    solves = [functools.partial(solved_terms, k) for k in range(1, pairs_most + 1)]
    middle, to_pal, to_far = lax.switch(count - 1, solves, table, own, pal, far)

    from_pal = lax.ppermute(to_pal, RING, even_edges())
    answers = [functools.partial(answer, k, most) for k in lengths]
    from_far = lax.switch(length, answers, to_far)
    return finish(table, asked, middle, from_pal, from_far)


def solution(mesh):
    placed = (
        P(("grp", "orb"), "slab", None, None),
        P(),
        P(("grp", "orb"), None),
        P(("grp", "orb")),
    )
    return jax.shard_map(
        body,
        mesh=mesh,
        in_specs=placed,
        out_specs=P(("grp", "orb"), "slab", None, None),
        check_vma=False,
    )
```

```python
import functools

import jax
import jax.numpy as jnp
from jax import lax
from jax.experimental import pallas as pl
from jax.experimental.pallas import tpu as pltpu
from jax.sharding import PartitionSpec as P

PASSES = 8
DIAG = 6.25
THETA = 1.075
DELTA = 0.925

BOX = 64
LANES = 128
PAD = 16
ROWS = BOX + 2 * PAD
VMEM_BYTES = 40 * 1024 * 1024


def params():
    return pltpu.CompilerParams(vmem_limit_bytes=VMEM_BYTES)


RING = ("grp", "orb")


def even_edges():
    return [(g, g ^ 1) for g in range(lax.axis_size(RING))]


def odd_edges():
    size = lax.axis_size(RING)
    return [(g, (g + 1 if g % 2 else g - 1) % size) for g in range(size)]


def lane_index(shape):
    return lax.broadcasted_iota(jnp.int32, shape, len(shape) - 1)


def moved_z(field, by):
    z = lane_index(field.shape) & (BOX - 1)
    source = z - by
    rolled = pltpu.roll(field, jnp.where(by < 0, by + LANES, by), 1)
    return jnp.where((source >= 0) & (source < BOX), rolled, 0.0)


def pack_kernel(field_ref, out_ref):
    half = field_ref.shape[1] // 2
    out_ref[...] = jnp.concatenate([field_ref[:, :half], field_ref[:, half:]], axis=-1)


def pack(orbitals):
    orbs, planes = orbitals.shape[:2]
    return pl.pallas_call(
        pack_kernel,
        grid=(2,),
        in_specs=[pl.BlockSpec((orbs // 2, planes, BOX, BOX), lambda i: (i, 0, 0, 0))],
        out_specs=pl.BlockSpec((orbs // 2, planes // 2, BOX, LANES), lambda i: (i, 0, 0, 0)),
        out_shape=jax.ShapeDtypeStruct((orbs, planes // 2, BOX, LANES), jnp.float32),
        compiler_params=params(),
    )(orbitals)


def finish_kernel(table_ref, asked_ref, mid_ref, pal_ref, far_ref, out_ref, acc):
    step, half = mid_ref.shape[:2]
    start = pl.program_id(0) * step
    orbs = pl.num_programs(0) * step
    acc[...] = mid_ref[...] + pal_ref[...]
    rank = 0
    for slot in range(asked_ref.shape[0]):
        local = asked_ref[slot] - orbs * table_ref[GROUP, 0]
        if slot:
            rank = jnp.minimum(rank, far_ref.shape[0] - 1)

        @pl.when((local >= start) & (local < start + step))
        def _():
            acc[local - start] += far_ref[rank]

        rank += ((local >= 0) & (local < orbs)).astype(jnp.int32)
    out_ref[:, :half] = acc[..., :BOX]
    out_ref[:, half:] = acc[..., BOX:]


def finish(table, asked, middle, from_pal, from_far):
    orbs, half = middle.shape[:2]
    step = 2
    smem = pl.BlockSpec(memory_space=pltpu.SMEM)
    spec = pl.BlockSpec((step, half, BOX, LANES), lambda i: (i, 0, 0, 0))
    return pl.pallas_call(
        finish_kernel,
        grid=(orbs // step,),
        in_specs=[smem, smem, spec, spec, pl.BlockSpec(memory_space=pltpu.VMEM)],
        out_specs=pl.BlockSpec((step, 2 * half, BOX, BOX), lambda i: (i, 0, 0, 0)),
        out_shape=jax.ShapeDtypeStruct((orbs, 2 * half, BOX, BOX), jnp.float32),
        scratch_shapes=[pltpu.VMEM((step, half, BOX, LANES), jnp.float32)],
        compiler_params=params(),
    )(table, asked, middle, from_pal, from_far)


def gather_kernel(table_ref, asked_ref, own_ref, out_ref, sems):
    orbs, count = own_ref.shape[0], out_ref.shape[0]
    chosen = [0] * count
    rank = 0
    for slot in range(asked_ref.shape[0]):
        local = asked_ref[slot] - orbs * table_ref[GROUP, 0]
        hit = (local >= 0) & (local < orbs)
        chosen = [jnp.where(hit & (rank == k), local, old) for k, old in enumerate(chosen)]
        rank += hit.astype(jnp.int32)
    copies = [
        pltpu.make_async_copy(own_ref.at[orb], out_ref.at[k], sems.at[k])
        for k, orb in enumerate(chosen)
    ]
    for copy in copies:
        copy.start()
    for copy in copies:
        copy.wait()


def gather(table, asked, own, count):
    smem = pl.BlockSpec(memory_space=pltpu.SMEM)
    anywhere = pl.BlockSpec(memory_space=pl.ANY)
    return pl.pallas_call(
        gather_kernel,
        in_specs=[smem, smem, anywhere],
        out_specs=anywhere,
        out_shape=jax.ShapeDtypeStruct((count,) + own.shape[1:], jnp.float32),
        scratch_shapes=[pltpu.SemaphoreType.DMA((count,))],
        compiler_params=params(),
    )(table, asked, own)


def spread_kernel(in_ref, out_ref, sem):
    copy = pltpu.make_async_copy(in_ref, out_ref.at[pl.ds(0, in_ref.shape[0])], sem)
    copy.start()
    copy.wait()


def spread(blocks, count):
    if blocks.shape[0] == count:
        return blocks
    anywhere = pl.BlockSpec(memory_space=pl.ANY)
    return pl.pallas_call(
        spread_kernel,
        in_specs=[anywhere],
        out_specs=anywhere,
        out_shape=jax.ShapeDtypeStruct((count,) + blocks.shape[1:], jnp.float32),
        scratch_shapes=[pltpu.SemaphoreType.DMA],
        compiler_params=params(),
    )(blocks)


def ask(count, most, table, asked, own):
    return spread(lax.ppermute(gather(table, asked, own, count), RING, odd_edges()), most)


def answer(count, most, terms):
    return spread(lax.ppermute(terms[:count], RING, odd_edges()), most)


FIRST, SECOND, BY_Y, BY_Z, GROUP, SLAB = range(6)
MINE, PAL, FAR = range(3)


def locate(table_ref, where_ref, orbs):
    group = table_ref[GROUP, 0]
    rank = 0
    for slot in range(where_ref.shape[1]):
        second = table_ref[SECOND, slot]
        mine = second - orbs * group
        other = second - orbs * (group ^ 1)
        is_mine = (mine >= 0) & (mine < orbs)
        is_pal = (other >= 0) & (other < orbs)
        is_far = (second >= 0) & ~is_mine & ~is_pal
        where_ref[0, slot] = jnp.where(is_pal, PAL, jnp.where(is_far, FAR, MINE))
        place = jnp.where(is_pal, other, jnp.where(is_far, rank, 0))
        where_ref[1, slot] = jnp.where(is_mine, mine, place)
        rank += is_far.astype(jnp.int32)


def clear_edges(padded):
    for x in range(padded.shape[0]):
        padded[x, :PAD] = jnp.zeros((PAD, LANES), jnp.float32)
        padded[x, PAD + BOX :] = jnp.zeros((PAD, LANES), jnp.float32)


def swapped(field):
    return pltpu.roll(field, LANES // 2, 1)


def density_kernel(table_ref, own_ref, pal_ref, far_ref, partner_ref, *rest):
    out_refs, (padded, where) = rest[:-2], rest[-2:]
    planes = own_ref.shape[1]
    locate(table_ref, where, own_ref.shape[0])
    clear_edges(padded)
    low = lane_index((BOX, LANES)) < BOX

    def place_partner(slot):
        for kind, ref in ((MINE, own_ref), (PAL, pal_ref), (FAR, far_ref)):

            @pl.when(where[0, slot] == kind)
            def _():
                padded[:, PAD : PAD + BOX] = ref[where[1, slot]]

        rows = pl.ds(PAD - table_ref[BY_Y, slot], BOX)
        for x in range(planes):
            partner_ref[slot, x] = moved_z(padded[x, rows, :], table_ref[BY_Z, slot])

    done = 0
    for out_ref in out_refs:
        count = out_ref.shape[0]

        @pl.loop(0, count)
        def _(pair):
            slot = 2 * (done + pair)
            place_partner(slot)
            place_partner(slot + 1)
            for x in range(planes):
                one = own_ref[table_ref[FIRST, slot], x] * partner_ref[slot, x]
                two = own_ref[table_ref[FIRST, slot + 1], x] * partner_ref[slot + 1, x]
                out_ref[pair, x] = jnp.where(low, one, swapped(two))
                out_ref[pair, planes + x] = jnp.where(low, swapped(one), two)

        done += count


def densities(table, own, pal, far, chunks):
    planes = own.shape[1]
    vmem = pl.BlockSpec(memory_space=pltpu.VMEM)
    shapes = [(2 * sum(chunks), planes, BOX, LANES)]
    shapes += [(count, 2 * planes, BOX, LANES) for count in chunks]
    return pl.pallas_call(
        density_kernel,
        in_specs=[pl.BlockSpec(memory_space=pltpu.SMEM)] + [vmem] * 3,
        out_specs=[vmem] * len(shapes),
        out_shape=[jax.ShapeDtypeStruct(shape, jnp.float32) for shape in shapes],
        scratch_shapes=[
            pltpu.VMEM((planes, ROWS, LANES), jnp.float32),
            pltpu.SMEM((2, table.shape[1]), jnp.int32),
        ],
        compiler_params=params(),
    )(table, own, pal, far)


def exchange_kernel(table_ref, own_ref, partner_ref, *rest):
    pot_refs = rest[:-5]
    mid_ref, to_pal_ref, to_far_ref, padded, where = rest[-5:]
    orbs, planes = mid_ref.shape[:2]
    locate(table_ref, where, orbs)
    clear_edges(padded)
    zeros = jnp.zeros((planes, BOX, LANES), jnp.float32)
    low = lane_index((BOX, LANES)) < BOX

    @pl.loop(0, orbs)
    def _(orb):
        mid_ref[orb] = zeros
        to_pal_ref[orb] = zeros

    def add_terms(slot, potential):
        first = table_ref[FIRST, slot]
        by_y = table_ref[BY_Y, slot]
        by_z = table_ref[BY_Z, slot]
        weight = jnp.where(table_ref[SECOND, slot] >= 0, 1.0, 0.0)
        for x in range(planes):
            pot = weight * potential(x)
            mid_ref[first, x] += pot * partner_ref[slot, x]
            padded[x, PAD : PAD + BOX] = moved_z(pot * own_ref[first, x], -by_z)
        rows = pl.ds(PAD + by_y, BOX)
        at = where[1, slot]

        @pl.when(where[0, slot] == MINE)
        def _():
            mid_ref[at] += padded[:, rows, :]

        @pl.when(where[0, slot] == PAL)
        def _():
            to_pal_ref[at] += padded[:, rows, :]

        @pl.when(where[0, slot] == FAR)
        def _():
            to_far_ref[at] = padded[:, rows, :]

    done = 0
    for pot_ref in pot_refs:
        count = pot_ref.shape[0]

        @pl.loop(0, count)
        def _(pair):
            slot = 2 * (done + pair)
            add_terms(
                slot,
                lambda x: jnp.where(low, pot_ref[pair, x], swapped(pot_ref[pair, planes + x])),
            )
            add_terms(
                slot + 1,
                lambda x: jnp.where(low, swapped(pot_ref[pair, x]), pot_ref[pair, planes + x]),
            )

        done += count


def exchange_terms(table, potentials, own, partner, most):
    planes = own.shape[1]
    vmem = pl.BlockSpec(memory_space=pltpu.VMEM)
    return pl.pallas_call(
        exchange_kernel,
        in_specs=[pl.BlockSpec(memory_space=pltpu.SMEM)] + [vmem] * (2 + len(potentials)),
        out_specs=[vmem] * 3,
        out_shape=[
            jax.ShapeDtypeStruct((count,) + own.shape[1:], jnp.float32)
            for count in (own.shape[0], own.shape[0], most)
        ],
        scratch_shapes=[
            pltpu.VMEM((planes, ROWS, LANES), jnp.float32),
            pltpu.SMEM((2, table.shape[1]), jnp.int32),
        ],
        compiler_params=params(),
    )(table, own, partner, *potentials)


SUB = 8


def coefficients():
    sigma = THETA / DELTA
    coef = 1.0 / sigma
    made = []
    for _ in range(PASSES - 1):
        new = 1.0 / (2.0 * sigma - coef)
        made.append((new * coef, 2.0 * new / (DELTA * DIAG)))
        coef = new
    return made


def solve_kernel(slabs, table_ref, far_ref, own_ref, near_ref, out_ref, dens, even, odd):
    slab = table_ref[SLAB, 0]
    pairs, planes = own_ref.shape[:2]
    flip = lax.rem(slab, 2)
    far_at = flip * 2 * planes
    near_at = (1 - flip) * 2 * planes
    z = lane_index((SUB, SUB, LANES)) & (BOX - 1)
    not_first = z > 0
    not_last = z < BOX - 1
    row = lax.broadcasted_iota(jnp.int32, (SUB, LANES), 0)
    below_in = jnp.where(slab > 0, 1.0, 0.0)
    above_in = jnp.where(slab < slabs - 1, 1.0, 0.0)
    core = slice(1, 1 + SUB)

    def put(buf, x, block):
        buf[x, core] = block
        buf[x, 0] = jnp.where(row > 0, pltpu.roll(block[SUB - 1], 1, 0), 0.0)
        buf[x, 1 + SUB] = jnp.where(row < SUB - 1, pltpu.roll(block[0], SUB - 1, 0), 0.0)

    def take(ref, pair, x):
        return jnp.stack([ref[pair, x, pl.ds(t, SUB, stride=SUB), :] for t in range(SUB)])

    @pl.loop(0, pairs)
    def _(pair):
        for x in range(planes):
            put(dens, far_at + x, take(far_ref, pair, x))
            put(dens, planes + x, take(own_ref, pair, x))
            put(dens, near_at + x, take(near_ref, pair, x))
        start = 1.0 / (DIAG * THETA)
        for turn, (keep, add) in enumerate(coefficients(), 1):
            source = dens if turn == 1 else (even if turn % 2 else odd)
            target = odd if turn % 2 else even
            here = 1.0 + keep - DIAG * add
            for x in range(turn + 1, 3 * planes - 1 - turn):
                mid = source[x, core]
                near = source[x - 1, core] + source[x + 1, core]
                near = near + (source[x, :SUB] + source[x, 2 : 2 + SUB])
                near = near + jnp.where(not_first, pltpu.roll(mid, 1, 2), 0.0)
                near = near + jnp.where(not_last, pltpu.roll(mid, LANES - 1, 2), 0.0)
                if turn == 1:
                    fresh = (here * start + add) * mid + (add * start) * near
                elif turn == 2:
                    fresh = here * mid + (add - keep * start) * dens[x, core] + add * near
                else:
                    fresh = here * mid - keep * target[x, core] + add * (near + dens[x, core])
                if x < planes:
                    fresh = fresh * below_in
                if x >= 2 * planes:
                    fresh = fresh * above_in
                if turn < PASSES - 1:
                    put(target, x, fresh)
                else:
                    for t in range(SUB):
                        out_ref[pair, x - planes, pl.ds(t, SUB, stride=SUB), :] = fresh[t]


def solve(table, far, own, near, slabs):
    planes = own.shape[1]
    vmem = pl.BlockSpec(memory_space=pltpu.VMEM)
    return pl.pallas_call(
        functools.partial(solve_kernel, slabs),
        in_specs=[pl.BlockSpec(memory_space=pltpu.SMEM), vmem, vmem, vmem],
        out_specs=vmem,
        out_shape=jax.ShapeDtypeStruct(own.shape, jnp.float32),
        scratch_shapes=[pltpu.VMEM((3 * planes, SUB + 2, SUB, LANES), jnp.float32)] * 3,
        compiler_params=params(),
    )(table, far, own, near)


def slot_table(offsets, pairs, seconds, orb_dev):
    total_orbs = offsets.shape[0]
    group = lax.axis_index(RING).astype(jnp.int32)
    ids = jnp.arange(total_orbs, dtype=jnp.int32)
    pick_first = (pairs[:, 0:1] == ids[None, :]).astype(jnp.int32)
    pick_second = (pairs[:, 1:2] == ids[None, :]).astype(jnp.int32)
    shift = jnp.sum((pick_second - pick_first)[:, :, None] * offsets[None, :, :], axis=1)
    constants = jnp.stack([group, lax.axis_index("slab").astype(jnp.int32)])
    return jnp.concatenate(
        [
            (pairs[:, 0] - orb_dev * group)[None, :],
            seconds[None, :],
            shift.T,
            jnp.broadcast_to(constants[:, None], (2, pairs.shape[0])),
        ],
        axis=0,
    )


def asked_by(seconds, group, orb_dev):
    local = seconds - orb_dev * group
    return jnp.sum(((local >= 0) & (local < orb_dev)).astype(jnp.int32))


def solved_terms(count, table, own, pal, far):
    slabs = lax.axis_size("slab")
    across = [(s, s ^ 1) for s in range(slabs)]
    onward = [(s, s + 2 - 4 * (s % 2)) for s in range(slabs)]
    onward = [(s, t) for s, t in onward if 0 <= t < slabs]
    partner, *made = densities(table, own, pal, far, [1] * count)
    near = [lax.ppermute(dens, "slab", across) for dens in made]
    next_but_one = [lax.ppermute(dens, "slab", onward) for dens in near]
    potentials = [solve(table, f, d, n, slabs) for f, d, n in zip(next_but_one, made, near)]
    return exchange_terms(table, potentials, own, partner, far.shape[0])


def body(orbitals, offsets, pairs, live):
    orbs, slots = orbitals.shape[0], live.shape[0]
    seconds = jnp.where(live > 0, pairs[:, 1], -1)
    asked = lax.ppermute(seconds, RING, odd_edges())
    own = pack(orbitals)
    offered, asked = lax.optimization_barrier((own, asked))
    pal = lax.ppermute(offered, RING, even_edges())
    table = slot_table(offsets, pairs, seconds, orbs)

    group = lax.axis_index(RING)
    beyond = (group + 2 * (group % 2) - 1) % lax.axis_size(RING)
    most = slots - 1
    longer = jnp.maximum(asked_by(asked, group, orbs), asked_by(seconds, beyond, orbs))
    length = jnp.clip(longer, 1, most) - 1
    lengths = range(1, most + 1)
    asks = [functools.partial(ask, k, most) for k in lengths]
    far = lax.switch(length, asks, table, asked, own)

    pairs_most = (slots + 1) // 2
    count = jnp.clip((jnp.sum(live) + 1) // 2, 1, pairs_most)
    solves = [functools.partial(solved_terms, k) for k in range(1, pairs_most + 1)]
    middle, to_pal, to_far = lax.switch(count - 1, solves, table, own, pal, far)

    from_pal = lax.ppermute(to_pal, RING, even_edges())
    answers = [functools.partial(answer, k, most) for k in lengths]
    from_far = lax.switch(length, answers, to_far)
    return finish(table, asked, middle, from_pal, from_far)


def solution(mesh):
    placed = (
        P(("grp", "orb"), "slab", None, None),
        P(),
        P(("grp", "orb"), None),
        P(("grp", "orb")),
    )
    return jax.shard_map(
        body,
        mesh=mesh,
        in_specs=placed,
        out_specs=P(("grp", "orb"), "slab", None, None),
        check_vma=False,
    )
```

```python
import functools

import jax
import jax.numpy as jnp
from jax import lax
from jax.experimental import pallas as pl
from jax.experimental.pallas import tpu as pltpu
from jax.sharding import PartitionSpec as P

PASSES = 8
DIAG = 6.25
THETA = 1.075
DELTA = 0.925

BOX = 64
LANES = 128
PAD = 16
ROWS = BOX + 2 * PAD
VMEM_BYTES = 40 * 1024 * 1024


def params():
    return pltpu.CompilerParams(vmem_limit_bytes=VMEM_BYTES)


RING = ("grp", "orb")


def group_index():
    return lax.axis_index("grp") * lax.axis_size("orb") + lax.axis_index("orb")


def even_edges():
    return [(g, g ^ 1) for g in range(lax.axis_size(RING))]


def odd_edges():
    size = lax.axis_size(RING)
    return [(g, (g + 1 if g % 2 else g - 1) % size) for g in range(size)]


def lane_index(shape):
    return lax.broadcasted_iota(jnp.int32, shape, len(shape) - 1)


def moved_z(field, by):
    z = lane_index(field.shape) & (BOX - 1)
    source = z - by
    rolled = pltpu.roll(field, jnp.where(by < 0, by + LANES, by), 1)
    return jnp.where((source >= 0) & (source < BOX), rolled, 0.0)


def cost(microseconds):
    return pl.CostEstimate(flops=0, bytes_accessed=int(3.6e6 * microseconds), transcendentals=0)


def pack_kernel(field_ref, out_ref):
    half = field_ref.shape[1] // 2
    out_ref[...] = jnp.concatenate([field_ref[:, :half], field_ref[:, half:]], axis=-1)


def pack(orbitals):
    orbs, planes = orbitals.shape[:2]
    return pl.pallas_call(
        pack_kernel,
        grid=(2,),
        in_specs=[pl.BlockSpec((orbs // 2, planes, BOX, BOX), lambda i: (i, 0, 0, 0))],
        out_specs=pl.BlockSpec((orbs // 2, planes // 2, BOX, LANES), lambda i: (i, 0, 0, 0)),
        out_shape=jax.ShapeDtypeStruct((orbs, planes // 2, BOX, LANES), jnp.float32),
        compiler_params=params(),
    )(orbitals)


def finish_kernel(asked_ref, mid_ref, pal_ref, far_ref, out_ref, acc):
    step, half = mid_ref.shape[:2]
    start = pl.program_id(0) * step
    orbs = pl.num_programs(0) * step
    acc[...] = mid_ref[...] + pal_ref[...]
    rank = 0
    for slot in range(asked_ref.shape[0]):
        local = asked_ref[slot] - orbs * group_index()
        if slot:
            rank = jnp.minimum(rank, far_ref.shape[0] - 1)

        @pl.when((local >= start) & (local < start + step))
        def _():
            acc[local - start] += far_ref[rank]

        rank += ((local >= 0) & (local < orbs)).astype(jnp.int32)
    out_ref[:, :half] = acc[..., :BOX]
    out_ref[:, half:] = acc[..., BOX:]


def finish(asked, middle, from_pal, from_far):
    orbs, half = middle.shape[:2]
    step = 2
    smem = pl.BlockSpec(memory_space=pltpu.SMEM)
    spec = pl.BlockSpec((step, half, BOX, LANES), lambda i: (i, 0, 0, 0))
    return pl.pallas_call(
        finish_kernel,
        grid=(orbs // step,),
        in_specs=[smem, spec, spec, pl.BlockSpec(memory_space=pltpu.VMEM)],
        out_specs=pl.BlockSpec((step, 2 * half, BOX, BOX), lambda i: (i, 0, 0, 0)),
        out_shape=jax.ShapeDtypeStruct((orbs, 2 * half, BOX, BOX), jnp.float32),
        scratch_shapes=[pltpu.VMEM((step, half, BOX, LANES), jnp.float32)],
        compiler_params=params(),
    )(asked, middle, from_pal, from_far)


def gather_kernel(asked_ref, own_ref, out_ref, sems):
    orbs, count = own_ref.shape[0], out_ref.shape[0]
    chosen = [0] * count
    rank = 0
    for slot in range(asked_ref.shape[0]):
        local = asked_ref[slot] - orbs * group_index()
        hit = (local >= 0) & (local < orbs)
        chosen = [jnp.where(hit & (rank == k), local, old) for k, old in enumerate(chosen)]
        rank += hit.astype(jnp.int32)
    copies = [
        pltpu.make_async_copy(own_ref.at[orb], out_ref.at[k], sems.at[k])
        for k, orb in enumerate(chosen)
    ]
    for copy in copies:
        copy.start()
    for copy in copies:
        copy.wait()


def gather(asked, own, count):
    smem = pl.BlockSpec(memory_space=pltpu.SMEM)
    anywhere = pl.BlockSpec(memory_space=pl.ANY)
    return pl.pallas_call(
        gather_kernel,
        in_specs=[smem, anywhere],
        out_specs=anywhere,
        out_shape=jax.ShapeDtypeStruct((count,) + own.shape[1:], jnp.float32),
        scratch_shapes=[pltpu.SemaphoreType.DMA((count,))],
        compiler_params=params(),
    )(asked, own)


def spread_kernel(in_ref, out_ref, sem):
    copy = pltpu.make_async_copy(in_ref, out_ref.at[pl.ds(0, in_ref.shape[0])], sem)
    copy.start()
    copy.wait()


def spread(blocks, count):
    if blocks.shape[0] == count:
        return blocks
    anywhere = pl.BlockSpec(memory_space=pl.ANY)
    return pl.pallas_call(
        spread_kernel,
        in_specs=[anywhere],
        out_specs=anywhere,
        out_shape=jax.ShapeDtypeStruct((count,) + blocks.shape[1:], jnp.float32),
        scratch_shapes=[pltpu.SemaphoreType.DMA],
        compiler_params=params(),
    )(blocks)


def ask(count, most, asked, own):
    return spread(lax.ppermute(gather(asked, own, count), RING, odd_edges()), most)


def answer(count, most, terms):
    return spread(lax.ppermute(terms[:count], RING, odd_edges()), most)


MINE, PAL, FAR = range(3)


class Slots:
    def __init__(self, pairs_ref, seconds_ref, offsets_ref, orbs):
        self.pairs, self.seconds, self.offsets, self.orbs = pairs_ref, seconds_ref, offsets_ref, orbs

    def first(self, slot):
        return self.pairs[0, slot] - self.orbs * group_index()

    def shift(self, axis, slot):
        return self.offsets[axis, self.pairs[1, slot]] - self.offsets[axis, self.pairs[0, slot]]


def locate(slots, where_ref):
    orbs, group = slots.orbs, group_index()
    rank = 0
    for slot in range(where_ref.shape[1]):
        second = slots.seconds[slot]
        mine = second - orbs * group
        other = second - orbs * (group ^ 1)
        is_mine = (mine >= 0) & (mine < orbs)
        is_pal = (other >= 0) & (other < orbs)
        is_far = (second >= 0) & ~is_mine & ~is_pal
        where_ref[0, slot] = jnp.where(is_pal, PAL, jnp.where(is_far, FAR, MINE))
        place = jnp.where(is_pal, other, jnp.where(is_far, rank, 0))
        where_ref[1, slot] = jnp.where(is_mine, mine, place)
        rank += is_far.astype(jnp.int32)


def clear_edges(padded):
    for x in range(padded.shape[0]):
        padded[x, :PAD] = jnp.zeros((PAD, LANES), jnp.float32)
        padded[x, PAD + BOX :] = jnp.zeros((PAD, LANES), jnp.float32)


def swapped(field):
    return pltpu.roll(field, LANES // 2, 1)


def density_kernel(pairs_ref, seconds_ref, offsets_ref, own_ref, pal_ref, far_ref, partner_ref, *rest):
    out_refs, (padded, where) = rest[:-2], rest[-2:]
    planes = own_ref.shape[1]
    slots = Slots(pairs_ref, seconds_ref, offsets_ref, own_ref.shape[0])
    locate(slots, where)
    clear_edges(padded)
    low = lane_index((BOX, LANES)) < BOX

    def place_partner(slot):
        for kind, ref in ((MINE, own_ref), (PAL, pal_ref), (FAR, far_ref)):

            @pl.when(where[0, slot] == kind)
            def _():
                padded[:, PAD : PAD + BOX] = ref[where[1, slot]]

        rows = pl.ds(PAD - slots.shift(0, slot), BOX)
        for x in range(planes):
            partner_ref[slot, x] = moved_z(padded[x, rows, :], slots.shift(1, slot))

    done = 0
    for out_ref in out_refs:
        count = out_ref.shape[0]

        @pl.loop(0, count)
        def _(pair):
            slot = 2 * (done + pair)
            place_partner(slot)
            place_partner(slot + 1)
            for x in range(planes):
                one = own_ref[slots.first(slot), x] * partner_ref[slot, x]
                two = own_ref[slots.first(slot + 1), x] * partner_ref[slot + 1, x]
                out_ref[pair, x] = jnp.where(low, one, swapped(two))
                out_ref[pair, planes + x] = jnp.where(low, swapped(one), two)

        done += count


def densities(tables, own, pal, far, chunks):
    planes = own.shape[1]
    vmem = pl.BlockSpec(memory_space=pltpu.VMEM)
    shapes = [(2 * sum(chunks), planes, BOX, LANES)]
    shapes += [(count, 2 * planes, BOX, LANES) for count in chunks]
    return pl.pallas_call(
        density_kernel,
        in_specs=[pl.BlockSpec(memory_space=pltpu.SMEM)] * 3 + [vmem] * 3,
        out_specs=[vmem] * len(shapes),
        out_shape=[jax.ShapeDtypeStruct(shape, jnp.float32) for shape in shapes],
        scratch_shapes=[
            pltpu.VMEM((planes, ROWS, LANES), jnp.float32),
            pltpu.SMEM((2, tables[1].shape[0]), jnp.int32),
        ],
        compiler_params=params(),
    )(*tables, own, pal, far)


def exchange_kernel(pairs_ref, seconds_ref, offsets_ref, own_ref, partner_ref, *rest):
    pot_refs = rest[:-5]
    mid_ref, to_pal_ref, to_far_ref, padded, where = rest[-5:]
    orbs, planes = mid_ref.shape[:2]
    slots = Slots(pairs_ref, seconds_ref, offsets_ref, orbs)
    locate(slots, where)
    clear_edges(padded)
    zeros = jnp.zeros((planes, BOX, LANES), jnp.float32)
    low = lane_index((BOX, LANES)) < BOX

    @pl.loop(0, orbs)
    def _(orb):
        mid_ref[orb] = zeros
        to_pal_ref[orb] = zeros

    def add_terms(slot, potential):
        first = slots.first(slot)
        by_y = slots.shift(0, slot)
        by_z = slots.shift(1, slot)
        weight = jnp.where(slots.seconds[slot] >= 0, 1.0, 0.0)
        for x in range(planes):
            pot = weight * potential(x)
            mid_ref[first, x] += pot * partner_ref[slot, x]
            padded[x, PAD : PAD + BOX] = moved_z(pot * own_ref[first, x], -by_z)
        rows = pl.ds(PAD + by_y, BOX)
        at = where[1, slot]

        @pl.when(where[0, slot] == MINE)
        def _():
            mid_ref[at] += padded[:, rows, :]

        @pl.when(where[0, slot] == PAL)
        def _():
            to_pal_ref[at] += padded[:, rows, :]

        @pl.when(where[0, slot] == FAR)
        def _():
            to_far_ref[at] = padded[:, rows, :]

    done = 0
    for pot_ref in pot_refs:
        count = pot_ref.shape[0]

        @pl.loop(0, count)
        def _(pair):
            slot = 2 * (done + pair)
            add_terms(
                slot,
                lambda x: jnp.where(low, pot_ref[pair, x], swapped(pot_ref[pair, planes + x])),
            )
            add_terms(
                slot + 1,
                lambda x: jnp.where(low, swapped(pot_ref[pair, x]), pot_ref[pair, planes + x]),
            )

        done += count


def exchange_terms(tables, potentials, own, partner, most):
    planes = own.shape[1]
    vmem = pl.BlockSpec(memory_space=pltpu.VMEM)
    return pl.pallas_call(
        exchange_kernel,
        in_specs=[pl.BlockSpec(memory_space=pltpu.SMEM)] * 3 + [vmem] * (2 + len(potentials)),
        out_specs=[vmem] * 3,
        out_shape=[
            jax.ShapeDtypeStruct((count,) + own.shape[1:], jnp.float32)
            for count in (own.shape[0], own.shape[0], most)
        ],
        scratch_shapes=[
            pltpu.VMEM((planes, ROWS, LANES), jnp.float32),
            pltpu.SMEM((2, tables[1].shape[0]), jnp.int32),
        ],
        compiler_params=params(),
    )(*tables, own, partner, *potentials)


SUB = 8


def coefficients():
    sigma = THETA / DELTA
    coef = 1.0 / sigma
    made = []
    for _ in range(PASSES - 1):
        new = 1.0 / (2.0 * sigma - coef)
        made.append((new * coef, 2.0 * new / (DELTA * DIAG)))
        coef = new
    return made


def solve_kernel(slabs, far_ref, own_ref, near_ref, out_ref, dens, even, odd):
    slab = lax.axis_index("slab")
    pairs, planes = own_ref.shape[:2]
    flip = lax.rem(slab, 2)
    far_at = flip * 2 * planes
    near_at = (1 - flip) * 2 * planes
    z = lane_index((SUB, SUB, LANES)) & (BOX - 1)
    not_first = z > 0
    not_last = z < BOX - 1
    row = lax.broadcasted_iota(jnp.int32, (SUB, LANES), 0)
    below_in = jnp.where(slab > 0, 1.0, 0.0)
    above_in = jnp.where(slab < slabs - 1, 1.0, 0.0)
    core = slice(1, 1 + SUB)

    def put(buf, x, block):
        buf[x, core] = block
        buf[x, 0] = jnp.where(row > 0, pltpu.roll(block[SUB - 1], 1, 0), 0.0)
        buf[x, 1 + SUB] = jnp.where(row < SUB - 1, pltpu.roll(block[0], SUB - 1, 0), 0.0)

    def take(ref, pair, x):
        return jnp.stack([ref[pair, x, pl.ds(t, SUB, stride=SUB), :] for t in range(SUB)])

    @pl.loop(0, pairs)
    def _(pair):
        for x in range(planes):
            put(dens, far_at + x, take(far_ref, pair, x))
            put(dens, planes + x, take(own_ref, pair, x))
            put(dens, near_at + x, take(near_ref, pair, x))
        start = 1.0 / (DIAG * THETA)
        for turn, (keep, add) in enumerate(coefficients(), 1):
            source = dens if turn == 1 else (even if turn % 2 else odd)
            target = odd if turn % 2 else even
            here = 1.0 + keep - DIAG * add
            for x in range(turn + 1, 3 * planes - 1 - turn):
                mid = source[x, core]
                near = source[x - 1, core] + source[x + 1, core]
                near = near + (source[x, :SUB] + source[x, 2 : 2 + SUB])
                near = near + jnp.where(not_first, pltpu.roll(mid, 1, 2), 0.0)
                near = near + jnp.where(not_last, pltpu.roll(mid, LANES - 1, 2), 0.0)
                if turn == 1:
                    fresh = (here * start + add) * mid + (add * start) * near
                elif turn == 2:
                    fresh = here * mid + (add - keep * start) * dens[x, core] + add * near
                else:
                    fresh = here * mid - keep * target[x, core] + add * (near + dens[x, core])
                if x < planes:
                    fresh = fresh * below_in
                if x >= 2 * planes:
                    fresh = fresh * above_in
                if turn < PASSES - 1:
                    put(target, x, fresh)
                else:
                    for t in range(SUB):
                        out_ref[pair, x - planes, pl.ds(t, SUB, stride=SUB), :] = fresh[t]


def solve(far, own, near, slabs):
    planes = own.shape[1]
    vmem = pl.BlockSpec(memory_space=pltpu.VMEM)
    return pl.pallas_call(
        functools.partial(solve_kernel, slabs),
        in_specs=[vmem] * 3,
        out_specs=vmem,
        out_shape=jax.ShapeDtypeStruct(own.shape, jnp.float32),
        scratch_shapes=[pltpu.VMEM((3 * planes, SUB + 2, SUB, LANES), jnp.float32)] * 3,
        cost_estimate=cost(own.shape[0] * 2.5),
        compiler_params=params(),
    )(far, own, near)


def asked_by(seconds, group, orb_dev):
    local = seconds - orb_dev * group
    return jnp.sum(((local >= 0) & (local < orb_dev)).astype(jnp.int32))


def solved_terms(count, tables, own, pal, far):
    slabs = lax.axis_size("slab")
    across = [(s, s ^ 1) for s in range(slabs)]
    onward = [(s, s + 2 - 4 * (s % 2)) for s in range(slabs)]
    onward = [(s, t) for s, t in onward if 0 <= t < slabs]
    partner, *made = densities(tables, own, pal, far, [1] * count)
    near = [lax.ppermute(dens, "slab", across) for dens in made]
    next_but_one = [lax.ppermute(dens, "slab", onward) for dens in near]
    potentials = [solve(f, d, n, slabs) for f, d, n in zip(next_but_one, made, near)]
    return exchange_terms(tables, potentials, own, partner, far.shape[0])


def body(orbitals, offsets, pairs, live):
    orbs, slots = orbitals.shape[0], live.shape[0]
    seconds = jnp.where(live > 0, pairs[:, 1], -1)
    asked = lax.ppermute(seconds, RING, odd_edges())
    own = pack(orbitals)
    offered, asked = lax.optimization_barrier((own, asked))
    pal = lax.ppermute(offered, RING, even_edges())
    tables = (pairs.T, seconds, offsets.T)

    group = lax.axis_index(RING)
    beyond = (group + 2 * (group % 2) - 1) % lax.axis_size(RING)
    most = slots - 1
    longer = jnp.maximum(asked_by(asked, group, orbs), asked_by(seconds, beyond, orbs))
    length = jnp.clip(longer, 1, most) - 1
    lengths = range(1, most + 1)
    asks = [functools.partial(ask, k, most) for k in lengths]
    far = lax.switch(length, asks, asked, own)

    pairs_most = (slots + 1) // 2
    count = jnp.clip((jnp.sum(live) + 1) // 2, 1, pairs_most)
    solves = [functools.partial(solved_terms, k) for k in range(1, pairs_most + 1)]
    middle, to_pal, to_far = lax.switch(count - 1, solves, tables, own, pal, far)

    from_pal = lax.ppermute(to_pal, RING, even_edges())
    answers = [functools.partial(answer, k, most) for k in lengths]
    from_far = lax.switch(length, answers, to_far)
    return finish(asked, middle, from_pal, from_far)


def solution(mesh):
    placed = (
        P(("grp", "orb"), "slab", None, None),
        P(),
        P(("grp", "orb"), None),
        P(("grp", "orb")),
    )
    return jax.shard_map(
        body,
        mesh=mesh,
        in_specs=placed,
        out_specs=P(("grp", "orb"), "slab", None, None),
        check_vma=False,
    )
```
